32 devices in a mesh: grp: 2 (over y), ffn: 4 (over z), hid: 4 (over x, core).
Axes of the slice: x: 2, y: 2, z: 4, core: 2. Of those that a mesh axis runs over, the one named last changes fastest.
Arguments:
- tokens: bfloat16 [4096, 18432], P(('grp', 'ffn'), 'hid'), parts along dimension 0, may hold values from -6 to 6
- query_weight: bfloat16 [18432, 8192], P('hid', 'ffn'), may hold values from -0.046875 to 0.046875
- kv_weight: bfloat16 [18432, 512], P('hid', 'ffn'), may hold values from -0.046875 to 0.046875
Outputs:
- attended: bfloat16 [4096, 8192], P(('grp', 'hid'), 'ffn'), parts along dimension 0
The draws below stay inside these ranges and needn't reach their ends.
There are 2 independent parts, one for each index of `grp`. The reference program is written for one: setup_inputs(seed, part) draws one part's arguments, and reference() takes and returns one part's arrays. A program takes and returns all parts, laid end to end along the dimension named above; an argument that names none is the same for every part. Nothing has to cross between parts.
All inputs are finite; a program needn't handle non-finite values.
Results may differ from the reference program's by a relative error of at most 0.0089.
Values may be sent and summed in bfloat16 or wider, within the bound.
No kernel may reach another device: no remote copies, remote signals or barrier semaphores. Data moves between devices by JAX's collectives and lax.ppermute only.
A program may use at most 192 MiB of HBM per device.

```python
import jax
import jax.numpy as jnp
from jax import lax

D = 18432
HEADS = 32
HEAD_DIM = 256
SEQ = 1024
TOKENS = 2048


def block_levels(own_key, extent, shards, low, high):
    loudness, own = 1.0, jax.random.fold_in(own_key, 6)
    for axis_at, blocks in shards:
        heights = jnp.exp(jax.random.uniform(jax.random.fold_in(own, axis_at), (blocks,), jnp.float32, low / len(shards), high / len(shards)))
        loudness = loudness * jnp.repeat(heights, extent[axis_at] // blocks).reshape([-1 if axis == axis_at else 1 for axis in range(len(extent))])
    return loudness


def normal_values(own_key, dims, width, limit, split=(), kind=jnp.bfloat16):
    loudness = block_levels(own_key, dims, split, -0.22, 0.18) if split else 1.0
    drawn = jax.random.normal(own_key, dims, jnp.float32) * width * loudness
    return jnp.minimum(jnp.maximum(drawn, -limit), limit).astype(kind)


def setup_inputs(seed: int = 0, part: int = 0) -> dict:
    arg_keys = jax.random.split(jax.random.key(seed), 4)
    own_keys = jax.random.split(jax.random.fold_in(arg_keys[3], part), 4)
    return {
        "tokens": normal_values(own_keys[0], (TOKENS, D), 1.0, 6.0, ((0, 4), (1, 4))),
        "query_weight": normal_values(arg_keys[1], (D, HEADS * HEAD_DIM), D ** -0.5, 0.046875, ((0, 4), (1, 4))),
        "kv_weight": normal_values(arg_keys[2], (D, 2 * HEAD_DIM), D ** -0.5, 0.046875, ((0, 4), (1, 4))),
    }


def reference(tokens, query_weight, kv_weight):
    queries = jnp.dot(tokens, query_weight, preferred_element_type=jnp.float32).astype(jnp.bfloat16)
    shared = jnp.dot(tokens, kv_weight, preferred_element_type=jnp.float32).astype(jnp.bfloat16)
    keys = shared[:, :HEAD_DIM]
    values = shared[:, HEAD_DIM:]
    position = jnp.arange(TOKENS, dtype=jnp.int32)
    same_prompt = (position[:, None] // SEQ) == (position[None, :] // SEQ)
    visible = same_prompt & (position[None, :] <= position[:, None])
    scale = HEAD_DIM ** -0.5
    per_head = jnp.transpose(queries.reshape(TOKENS, HEADS, HEAD_DIM), (1, 0, 2))

    def one_head(query_block):
        scores = jnp.dot(query_block, keys.T, preferred_element_type=jnp.float32) * scale
        weights = jnp.where(visible, jnp.exp(scores), jnp.float32(0.0))
        probs = (weights / jnp.sum(weights, axis=1, keepdims=True)).astype(jnp.bfloat16)
        return jnp.dot(probs, values, preferred_element_type=jnp.float32).astype(jnp.bfloat16)

    outputs = lax.map(one_head, per_head)
    return jnp.transpose(outputs, (1, 0, 2)).reshape(TOKENS, HEADS * HEAD_DIM)
```

```python
import functools

import jax
import jax.numpy as jnp
from jax import lax
from jax.experimental import pallas as pl
from jax.experimental.pallas import tpu as pltpu
from jax.sharding import PartitionSpec as P

HEAD_DIM = 256
SEQ = 1024
F32, BF16 = jnp.float32, jnp.bfloat16


def general(tokens, query_weight, kv_weight):
    local_rows = tokens.shape[0]
    total_rows = local_rows * lax.axis_size("ffn")
    query_count = total_rows // lax.axis_size("hid")
    heads_here = query_weight.shape[1] // HEAD_DIM
    kv_block = lax.all_gather(kv_weight, "ffn", axis=1, tiled=True)
    kv_partial = jnp.dot(tokens, kv_block, preferred_element_type=jnp.float32)
    kv_summed = lax.psum(kv_partial, "hid")
    shared = lax.all_gather(kv_summed.astype(jnp.bfloat16), "ffn", axis=0, tiled=True)
    keys = shared[:, :HEAD_DIM]
    values = shared[:, HEAD_DIM:]
    query_partial = jnp.dot(
        lax.all_gather(tokens, "ffn", axis=0, tiled=True),
        query_weight,
        preferred_element_type=jnp.float32,
    )
    query_summed = lax.psum_scatter(query_partial, "hid", scatter_dimension=0, tiled=True)
    queries = query_summed.astype(jnp.bfloat16)
    first_row = lax.axis_index("hid") * query_count
    query_pos = first_row + jnp.arange(query_count, dtype=jnp.int32)
    key_pos = jnp.arange(total_rows, dtype=jnp.int32)
    same_prompt = query_pos[:, None] // SEQ == key_pos[None, :] // SEQ
    visible = same_prompt & (key_pos[None, :] <= query_pos[:, None])
    scale = HEAD_DIM ** (-0.5)
    split_heads = queries.reshape(query_count, heads_here, HEAD_DIM)
    scores = (
        jnp.einsum("qhd,kd->hqk", split_heads, keys, preferred_element_type=jnp.float32) * scale
    )
    weights = jnp.where(visible[None, :, :], jnp.exp(scores), jnp.float32(0.0))
    probs = (weights / jnp.sum(weights, axis=2, keepdims=True)).astype(jnp.bfloat16)
    mixed = jnp.einsum("hqk,kd->qhd", probs, values, preferred_element_type=jnp.float32)
    return mixed.reshape(query_count, heads_here * HEAD_DIM).astype(jnp.bfloat16)


def attention_kernel(rows, where_ref, q_ref, kv_ref, o_ref):
    tile = rows // 2
    later = where_ref[0]
    scale = HEAD_DIM ** (-0.5) * 1.4426950408889634
    row = lax.broadcasted_iota(jnp.int32, (tile, tile), 0)
    col = lax.broadcasted_iota(jnp.int32, (tile, tile), 1)
    seen = col <= row

    def strip(first, count):
        q = q_ref[pl.ds(first * tile, tile), :]
        keys = kv_ref[: count * tile, :HEAD_DIM]
        values = kv_ref[: count * tile, HEAD_DIM:]
        s = lax.dot_general(q, keys, (((1,), (1,)), ((), ())), preferred_element_type=F32)
        last = jnp.where(seen, s[:, (count - 1) * tile :], -jnp.inf)
        s = last if count == 1 else jnp.concatenate([s[:, : (count - 1) * tile], last], axis=1)
        top = jnp.max(s, axis=1, keepdims=True)
        w = jnp.exp2((s - top) * scale)
        total = jnp.sum(w, axis=1, keepdims=True)
        mixed = jnp.dot(w.astype(BF16), values, preferred_element_type=F32)
        o_ref[pl.ds(first * tile, tile), :] = (mixed / total).astype(BF16)

    @pl.when(later == 0)
    def _():
        strip(0, 1)
        strip(1, 2)

    @pl.when(later == 1)
    def _():
        strip(0, 3)
        strip(1, 4)


def attention(later, queries, shared):
    rows, width = queries.shape
    return pl.pallas_call(
        functools.partial(attention_kernel, rows),
        out_shape=jax.ShapeDtypeStruct(queries.shape, BF16),
        grid_spec=pltpu.PrefetchScalarGridSpec(
            num_scalar_prefetch=1,
            grid=(width // HEAD_DIM,),
            in_specs=[
                pl.BlockSpec((rows, HEAD_DIM), lambda i, _: (0, i)),
                pl.BlockSpec(shared.shape, lambda i, _: (0, 0)),
            ],
            out_specs=pl.BlockSpec((rows, HEAD_DIM), lambda i, _: (0, i)),
        ),
        compiler_params=pltpu.CompilerParams(vmem_limit_bytes=32 * 2**20),
        cost_estimate=pl.CostEstimate(flops=6 * 10**9, bytes_accessed=5 * 10**6, transcendentals=3 * 10**6),
    )(later.reshape(1).astype(jnp.int32), queries, shared)


MID = [(1, 2), (2, 1)]
INTO = [(0, 1), (3, 2)]
OUT = [(1, 0), (2, 3)]
ORDER = ((0, 1, 2, 3), (1, 2, 1, 2), (2, 0, 3, 1), (3, 3, 0, 0))


def gate(xs, deps):
    deps = [x for x in deps if x is not None]
    return lax.optimization_barrier((tuple(xs), tuple(deps)))[0]


class Steps:
    def __init__(self):
        self.last, self.before, self.now, self.arrived = None, [], [], []

    def step(self):
        self.before, self.now = self.now, []

    def start(self, move, x):
        (x,) = gate((x,), (self.last,))
        self.now.append(move(x))
        return self.now[-1]

    def land(self):
        self.arrived = self.before

    def run(self, work, *xs):
        xs = gate(xs, [self.last] + self.arrived)
        out = work(*xs)
        self.last, self.arrived = jax.tree.leaves(out)[0], []
        return out


def to_core(x, blocks):
    pairs = []
    for z, block in enumerate(blocks):
        core = block % 2
        pairs += [(z * 4 + chip * 2 + 1 - core, z * 4 + chip * 2 + core) for chip in range(2)]
    return lax.ppermute(x, ("ffn", "hid"), pairs)


def to_chip(x, blocks):
    pairs = [(z * 4 + (block ^ 2), z * 4 + block) for z, block in enumerate(blocks)]
    return lax.ppermute(x, ("ffn", "hid"), pairs)


def to_end(x, blocks):
    pairs = [(z * 4 + blocks[z], end * 4 + blocks[z]) for z, end in OUT]
    return lax.ppermute(x, ("ffn", "hid"), pairs)


def gathered(x):
    z = lax.axis_index("ffn")
    got = [x] + [lax.ppermute(x, "ffn", [(i, i ^ k) for i in range(4)]) for k in (1, 2, 3)]
    columns = []
    for i in range(4):
        column = got[0]
        for k in (1, 2, 3):
            column = jnp.where((z ^ i) == k, got[k], column)
        columns.append(column)
    return jnp.concatenate(columns, 1)


TILE = 512


def product_kernel(terms, sums, kinds, heads, sp_ref, *refs):
    refs = list(refs)
    loaded = []
    for pieces, weights in terms:
        xs = [[refs.pop(0) for _ in range(n)] for n in pieces]
        if weights == "help":
            ws = [refs.pop(0) for _ in range(8)]
            loaded.append((xs, ws, None))
        else:
            ws = [refs.pop(0) for _ in weights]
            loaded.append((xs, ws, [refs.pop(0) for _ in weights]))
    outs = [[refs.pop(0) for _ in kinds] for _ in sums]
    kept = refs
    j = pl.program_id(0)
    inner = sp_ref[0] == 1

    @pl.when(j == 0)
    def _():
        for (xs, _, _), keep in zip(loaded, kept):
            at = 0
            for piece in xs:
                m = piece[0].shape[0]
                x = piece[0][...]
                if len(piece) == 2:
                    x = jnp.where(inner, x, piece[1][...])
                keep[pl.ds(at, m), :] = x
                at += m

    def total(chosen, part):
        acc = None
        for i in chosen:
            _, ws, kvs = loaded[i]
            at = 0
            for k, w in enumerate(ws):
                if part == "heads":
                    w = w[...]
                else:
                    w = w[:, : heads[1]] if kvs is None else kvs[k][...]
                x = kept[i][:, at : at + w.shape[0]]
                at += w.shape[0]
                y = jnp.dot(x, w, preferred_element_type=F32)
                acc = y if acc is None else acc + y
        return acc

    @pl.when(j < heads[0])
    def _():
        for chosen, out in zip(sums, outs):
            acc = total(chosen, "heads")
            for o in out:
                o[...] = acc.astype(o.dtype)

    @pl.when(j == heads[0])
    def _():
        for chosen, out in zip(sums, outs):
            acc = total(chosen, "kv")
            for o in out:
                o[:, : heads[1]] = acc.astype(o.dtype)


def product(sp, query_weight, kv_weight, terms, sums, kinds=(F32, BF16)):
    width, kv_width = query_weight.shape[1], kv_weight.shape[1]
    tiles = width // TILE
    args, specs, shape, scratch, flops = [], [], [], [], 0

    def own(at, size, columns, which):
        def index(j, sp):
            return (at if isinstance(at, int) else pl.multiple_of(sp[at[0]], 128), jnp.minimum(j, tiles - 1) * TILE if which else 0)

        return pl.BlockSpec((pl.Element(size), pl.Element(columns)), index)

    for pieces, weights in terms:
        for piece in pieces:
            for x in piece:
                args.append(x)
                specs.append(pl.BlockSpec(x.shape, lambda j, sp: (0, 0)))
        rows = sum(piece[0].shape[0] for piece in pieces)
        depth = pieces[0][0].shape[1]
        scratch.append(pltpu.VMEM((rows, depth), BF16))
        flops += 2 * rows * depth * (width + kv_width)
        if isinstance(weights[0], tuple):
            args += [query_weight] * len(weights) + [kv_weight] * len(weights)
            specs += [own(at, size, TILE, True) for at, size in weights]
            specs += [own(at, size, kv_width, False) for at, size in weights]
            shape.append((tuple(len(p) for p in pieces), tuple(weights)))
        else:
            args += list(weights)
            specs += [pl.BlockSpec((w.shape[0], TILE), lambda j, sp: (0, j)) for w in weights]
            shape.append((tuple(len(p) for p in pieces), "help"))
    rows = [scratch[chosen[0]].shape[0] for chosen in sums]
    out = pl.pallas_call(
        functools.partial(product_kernel, shape, sums, kinds, (tiles, kv_width)),
        out_shape=[jax.ShapeDtypeStruct((m, width + kv_width), k) for m in rows for k in kinds],
        grid_spec=pltpu.PrefetchScalarGridSpec(
            num_scalar_prefetch=1,
            grid=(tiles + 1,),
            in_specs=specs,
            out_specs=[pl.BlockSpec((m, TILE), lambda j, sp: (0, j)) for m in rows for _ in kinds],
            scratch_shapes=scratch,
        ),
        compiler_params=pltpu.CompilerParams(vmem_limit_bytes=48 * 2**20),
        cost_estimate=pl.CostEstimate(
            flops=flops // 2, bytes_accessed=flops // 1000, transcendentals=0
        ),
    )(sp, *args)
    out = [tuple(out[i : i + len(kinds)]) for i in range(0, len(out), len(kinds))]
    return out[0] if len(out) == 1 else out


def along(axis, pairs):
    return lambda x: lax.ppermute(x, axis, pairs)


def staged(tokens, query_weight, kv_weight):
    rows, depth = tokens.shape
    width = query_weight.shape[1]
    z, hid, grp = (lax.axis_index(name) for name in ("ffn", "hid", "grp"))
    inner = (z == 1) | (z == 2)
    part = depth * 2 // 9 // 128 * 128
    first = depth - 2 * part
    halves = ((0, rows // 2), (rows // 2, rows // 2))
    mid, into, out = along("ffn", MID), along("ffn", INTO), along("ffn", OUT)
    across = along("grp", [(0, 1), (1, 0)])
    core = [functools.partial(to_core, blocks=blocks) for blocks in ORDER]
    far = [functools.partial(to_chip, blocks=blocks) for blocks in ORDER]
    home = [functools.partial(to_end, blocks=blocks) for blocks in ORDER]

    own_at, far_at = first + grp * part, first + (1 - grp) * part
    sp = jnp.stack([inner.astype(jnp.int32), own_at, far_at]).astype(jnp.int32)
    weights1 = ((0, first),)
    weights2 = (((1,), part), ((2,), part))

    def both(x):
        return x, x.astype(BF16)

    def added(x, y):
        return both(x + y.astype(F32))

    def rounded(x, y):
        return (x + y.astype(F32)).astype(BF16)

    def make(terms, sums=((0, 1),)):
        return product(sp, query_weight, kv_weight, terms, sums)

    quarter = part // 4

    def weights_at(i):
        return jnp.concatenate(
            [
                lax.dynamic_slice_in_dim(w, own_at + i * quarter, quarter, 0)
                for w in (query_weight, kv_weight)
            ],
            1,
        )

    s = Steps()
    t1 = [tokens[a : a + m, :first] for a, m in halves]
    t2 = [
        jnp.concatenate(
            [lax.dynamic_slice(tokens, (a, at), (m, part)) for at in (own_at, far_at)], 1
        )
        for a, m in halves
    ]

    b1 = [s.start(mid, t1[0])]
    e1 = [s.start(out, t1[0])]
    w_in = [s.start(into, weights_at(0))]
    q_a, q_a16 = s.run(lambda x: make([([(x,)], ((0, depth),))], ((0,),)), tokens)
    s.step()
    b1.append(s.start(mid, t1[1]))
    e1.append(s.start(out, t1[1]))
    w_in.append(s.start(into, weights_at(1)))
    c_a = s.start(core[0], q_a16)
    s.land()
    w_far = [s.start(across, w_in[0])]
    f1 = [s.start(out, b1[0])]
    mark = s.run(lambda x, y: x[:16, :128] + y[:16, :128], b1[0], w_in[0])
    s.step()
    b2 = [s.start(mid, t2[0])]
    w_in.append(s.start(into, weights_at(2)))
    s.land()
    w_far.append(s.start(across, w_in[1]))
    f1.append(s.start(out, b1[1]))
    q_a, q_a16 = s.run(added, q_a, c_a)
    s.step()
    b2.append(s.start(mid, t2[1]))
    w_in.append(s.start(into, weights_at(3)))
    x_a = s.start(far[0], q_a16)
    s.land()
    w_far.append(s.start(across, w_in[2]))
    mark = s.run(lambda x, y: x[:16, :128] + y[:16, :128], b1[1], w_in[2])
    s.step()
    c1 = [s.start(into, t1[0])]
    s.land()
    w_far.append(s.start(across, w_in[3]))
    q_b, q_b16 = s.run(
        lambda *x: make([([(x[0], x[2]), (x[1], x[3])], weights1), ([(x[4],), (x[5],)], weights2)]),
        *b1, *e1, *b2,
    )
    s.step()
    c1.append(s.start(into, t1[1]))
    c_b = s.start(core[1], q_b16)
    s.land()
    d1 = [s.start(mid, c1[0])]
    help_ab = s.run(
        lambda *x: make(
            [([(x[0],), (x[1],)], x[4:]), ([(x[2],), (x[3],)], x[4:])], ((0,), (1,))
        ),
        *t2, *b2, *w_in, *w_far,
    )
    (h_a, h_a16), (h_b, h_b16) = help_ab
    s.step()
    c2 = [s.start(into, t2[0])]
    c_ha = s.start(core[0], h_a16)
    c_hb = s.start(core[1], h_b16)
    s.land()
    d1.append(s.start(mid, c1[1]))
    q_b, q_b16 = s.run(added, q_b, c_b)
    s.step()
    c2.append(s.start(into, t2[1]))
    x_b = s.start(far[1], q_b16)
    s.land()
    d2 = [s.start(mid, c2[0])]
    g1 = [s.start(out, d1[0])]
    h_a, h_a16 = s.run(added, h_a, c_ha)
    h_b, h_b16 = s.run(added, h_b, c_hb)
    s.step()
    x_ha = s.start(far[0], h_a16)
    x_hb = s.start(far[1], h_b16)
    s.land()
    d2.append(s.start(mid, c2[1]))
    g1.append(s.start(out, d1[1]))

    def last(*x):
        return make(
            [([(x[0], x[1])], weights1), ([(x[2],)], weights2), ([(x[2],)], x[3:])], ((2,), (0, 1))
        )

    (h_d0, h_d016), (q_d0, q_d016) = s.run(last, d1[0], g1[0], d2[0], *w_in, *w_far)
    q_c, q_c16 = s.run(
        lambda *x: make([([(x[0], x[2]), (x[1], x[3])], weights1), ([(x[4],), (x[5],)], weights2)]),
        *c1, *f1, *c2,
    )
    s.step()
    c_hd0 = s.start(core[3], h_d016)
    c_d0 = s.start(core[3], q_d016)
    c_c = s.start(core[2], q_c16)
    s.land()
    (h_d1, h_d116), (q_d1, q_d116) = s.run(last, d1[1], g1[1], d2[1], *w_in, *w_far)
    h_a = s.run(rounded, h_a, x_ha)
    h_b = s.run(rounded, h_b, x_hb)
    s.step()
    c_hd1 = s.start(core[3], h_d116)
    c_d1 = s.start(core[3], q_d116)
    o_ha = s.start(home[0], h_a)
    o_hb = s.start(home[1], h_b)
    s.land()
    h_d0, h_d016 = s.run(added, h_d0, c_hd0)
    q_d0, q_d016 = s.run(added, q_d0, c_d0)
    q_c, q_c16 = s.run(added, q_c, c_c)
    s.step()
    x_hd0 = s.start(far[3], h_d016)
    x_d0 = s.start(far[3], q_d016)
    x_c = s.start(far[2], q_c16)
    h_d1, h_d116 = added(h_d1, c_hd1)
    q_d1, q_d116 = added(q_d1, c_d1)
    x_hd1 = far[3](h_d116)
    x_d1 = far[3](q_d116)
    o_hd0 = home[3](rounded(h_d0, x_hd0))
    o_hd1 = home[3](rounded(h_d1, x_hd1))

    late = [
        (q + x.astype(F32) + o.astype(F32)).astype(BF16)
        for q, x, o in ((q_d0, x_d0, o_hd0), (q_d1, x_d1, o_hd1))
    ]
    block = jnp.concatenate(late, 0)
    stages = (
        q_a + x_a.astype(F32),
        q_b + x_b.astype(F32) + o_ha.astype(F32),
        q_c + x_c.astype(F32) + o_hb.astype(F32),
    )
    for stage, order in zip(stages, ORDER):
        here = sum(jnp.where(z == i, b, 0) for i, b in enumerate(order)) == hid
        block = jnp.where(here, stage.astype(BF16), block)
    kv_mine = gathered(block[:, width:])
    kv_other = lax.ppermute(kv_mine, "hid", [(i, i ^ 1) for i in range(4)])
    which = hid % 2
    shared = jnp.concatenate(
        [jnp.where(which == 0, kv_mine, kv_other), jnp.where(which == 0, kv_other, kv_mine)], 0
    )
    return attention(which, block[:, :width], shared)


def solution(mesh):
    fits = mesh.shape["ffn"] == 4 and mesh.shape["hid"] == 4 and mesh.shape["grp"] == 2
    return jax.shard_map(
        staged if fits else general,
        mesh=mesh,
        in_specs=(P(("grp", "ffn"), "hid"), P("hid", "ffn"), P("hid", "ffn")),
        out_specs=P(("grp", "hid"), "ffn"),
        check_vma=False,
    )
```

```python
import functools

import jax
import jax.numpy as jnp
from jax import lax
from jax.experimental import pallas as pl
from jax.experimental.pallas import tpu as pltpu
from jax.sharding import PartitionSpec as P

HEAD_DIM = 256
SEQ = 1024
F32, BF16 = jnp.float32, jnp.bfloat16


def general(tokens, query_weight, kv_weight):
    local_rows = tokens.shape[0]
    total_rows = local_rows * lax.axis_size("ffn")
    query_count = total_rows // lax.axis_size("hid")
    heads_here = query_weight.shape[1] // HEAD_DIM
    kv_block = lax.all_gather(kv_weight, "ffn", axis=1, tiled=True)
    kv_partial = jnp.dot(tokens, kv_block, preferred_element_type=jnp.float32)
    kv_summed = lax.psum(kv_partial, "hid")
    shared = lax.all_gather(kv_summed.astype(jnp.bfloat16), "ffn", axis=0, tiled=True)
    keys = shared[:, :HEAD_DIM]
    values = shared[:, HEAD_DIM:]
    query_partial = jnp.dot(
        lax.all_gather(tokens, "ffn", axis=0, tiled=True),
        query_weight,
        preferred_element_type=jnp.float32,
    )
    query_summed = lax.psum_scatter(query_partial, "hid", scatter_dimension=0, tiled=True)
    queries = query_summed.astype(jnp.bfloat16)
    first_row = lax.axis_index("hid") * query_count
    query_pos = first_row + jnp.arange(query_count, dtype=jnp.int32)
    key_pos = jnp.arange(total_rows, dtype=jnp.int32)
    same_prompt = query_pos[:, None] // SEQ == key_pos[None, :] // SEQ
    visible = same_prompt & (key_pos[None, :] <= query_pos[:, None])
    scale = HEAD_DIM ** (-0.5)
    split_heads = queries.reshape(query_count, heads_here, HEAD_DIM)
    scores = (
        jnp.einsum("qhd,kd->hqk", split_heads, keys, preferred_element_type=jnp.float32) * scale
    )
    weights = jnp.where(visible[None, :, :], jnp.exp(scores), jnp.float32(0.0))
    probs = (weights / jnp.sum(weights, axis=2, keepdims=True)).astype(jnp.bfloat16)
    mixed = jnp.einsum("hqk,kd->qhd", probs, values, preferred_element_type=jnp.float32)
    return mixed.reshape(query_count, heads_here * HEAD_DIM).astype(jnp.bfloat16)


def attention_kernel(rows, where_ref, q_ref, kv_ref, o_ref):
    tile = rows // 2
    later = where_ref[0]
    scale = HEAD_DIM ** (-0.5) * 1.4426950408889634
    row = lax.broadcasted_iota(jnp.int32, (tile, tile), 0)
    col = lax.broadcasted_iota(jnp.int32, (tile, tile), 1)
    seen = col <= row

    def strip(first, count):
        q = q_ref[pl.ds(first * tile, tile), :]
        keys = kv_ref[: count * tile, :HEAD_DIM]
        values = kv_ref[: count * tile, HEAD_DIM:]
        s = lax.dot_general(q, keys, (((1,), (1,)), ((), ())), preferred_element_type=F32)
        last = jnp.where(seen, s[:, (count - 1) * tile :], -jnp.inf)
        s = last if count == 1 else jnp.concatenate([s[:, : (count - 1) * tile], last], axis=1)
        top = jnp.max(s, axis=1, keepdims=True)
        w = jnp.exp2((s - top) * scale)
        total = jnp.sum(w, axis=1, keepdims=True)
        mixed = jnp.dot(w.astype(BF16), values, preferred_element_type=F32)
        o_ref[pl.ds(first * tile, tile), :] = (mixed / total).astype(BF16)

    @pl.when(later == 0)
    def _():
        strip(0, 1)
        strip(1, 2)

    @pl.when(later == 1)
    def _():
        strip(0, 3)
        strip(1, 4)


def attention(later, queries, shared):
    rows, width = queries.shape
    return pl.pallas_call(
        functools.partial(attention_kernel, rows),
        out_shape=jax.ShapeDtypeStruct(queries.shape, BF16),
        grid_spec=pltpu.PrefetchScalarGridSpec(
            num_scalar_prefetch=1,
            grid=(width // HEAD_DIM,),
            in_specs=[
                pl.BlockSpec((rows, HEAD_DIM), lambda i, _: (0, i)),
                pl.BlockSpec(shared.shape, lambda i, _: (0, 0)),
            ],
            out_specs=pl.BlockSpec((rows, HEAD_DIM), lambda i, _: (0, i)),
        ),
        compiler_params=pltpu.CompilerParams(vmem_limit_bytes=32 * 2**20),
        cost_estimate=pl.CostEstimate(flops=6 * 10**9, bytes_accessed=5 * 10**6, transcendentals=3 * 10**6),
    )(later.reshape(1).astype(jnp.int32), queries, shared)


def other_core(x):
    return lax.ppermute(x, "hid", [(i, i ^ 1) for i in range(4)])


def other_chip(x):
    return lax.ppermute(x, "hid", [(i, i ^ 2) for i in range(4)])


def gathered(x):
    z = lax.axis_index("ffn")
    got = [x] + [lax.ppermute(x, "ffn", [(i, i ^ k) for i in range(4)]) for k in (1, 2, 3)]
    columns = []
    for i in range(4):
        column = got[0]
        for k in (1, 2, 3):
            column = jnp.where((z ^ i) == k, got[k], column)
        columns.append(column)
    return jnp.concatenate(columns, 1)


TILE = 512
SHARES = (6, 6, 4)


def product_kernel(terms, sums, kinds, heads, based, sp_ref, *refs):
    refs = list(refs)
    base = refs.pop(0) if based else None
    loaded = []
    for pieces, weights in terms:
        xs = [[refs.pop(0) for _ in range(n)] for n in pieces]
        if weights == "help":
            ws = [refs.pop(0) for _ in range(8)]
            loaded.append((xs, ws, None))
        else:
            ws = [refs.pop(0) for _ in weights]
            loaded.append((xs, ws, [refs.pop(0) for _ in weights]))
    outs = [[refs.pop(0) for _ in kinds] for _ in sums]
    kept = refs
    j = pl.program_id(0)
    inner = sp_ref[0] == 1

    @pl.when(j == 0)
    def _():
        for (xs, _, _), keep in zip(loaded, kept):
            if len(xs) == 1 and len(xs[0]) == 1:
                continue
            at = 0
            for piece in xs:
                m = piece[0].shape[0]
                x = piece[0][...]
                if len(piece) == 2:
                    x = jnp.where(inner, x, piece[1][...])
                keep[pl.ds(at, m), :] = x
                at += m

    def total(chosen, part):
        acc = None
        if base is not None:
            acc = base[...] if part == "heads" else base[:, : heads[1]]
        for i in chosen:
            xs, ws, kvs = loaded[i]
            source = xs[0][0] if len(xs) == 1 and len(xs[0]) == 1 else kept[i]
            at = 0
            for k, w in enumerate(ws):
                if part == "heads":
                    w = w[...]
                else:
                    w = w[:, : heads[1]] if kvs is None else kvs[k][...]
                x = source[:, at : at + w.shape[0]]
                at += w.shape[0]
                y = jnp.dot(x, w, preferred_element_type=F32)
                acc = y if acc is None else acc + y
        return acc

    @pl.when(j < heads[0])
    def _():
        for chosen, out in zip(sums, outs):
            acc = total(chosen, "heads")
            for o in out:
                o[...] = acc.astype(o.dtype)

    @pl.when(j == heads[0])
    def _():
        for chosen, out in zip(sums, outs):
            acc = total(chosen, "kv")
            for o in out:
                o[:, : heads[1]] = acc.astype(o.dtype)


def product(sp, query_weight, kv_weight, terms, sums, kinds=(F32, BF16), base=None, base_at=0):
    width, kv_width = query_weight.shape[1], kv_weight.shape[1]
    tiles = width // TILE
    args, specs, shape, scratch = [], [], [], []

    def own(at, size, columns, which):
        def index(j, sp):
            return (at if isinstance(at, int) else pl.multiple_of(sp[at[0]], 128), jnp.minimum(j, tiles - 1) * TILE if which else 0)

        return pl.BlockSpec((pl.Element(size), pl.Element(columns)), index)

    if base is not None:
        m = sum(piece[0].shape[0] for piece in terms[0][0])
        args.append(base)
        specs.append(pl.BlockSpec((m, TILE), lambda j, sp: (base_at, j)))
    for pieces, weights in terms:
        for piece in pieces:
            for x in piece:
                args.append(x)
                specs.append(pl.BlockSpec(x.shape, lambda j, sp: (0, 0)))
        rows = sum(piece[0].shape[0] for piece in pieces)
        depth = pieces[0][0].shape[1]
        scratch.append(pltpu.VMEM((rows, depth), BF16))
        if isinstance(weights[0], tuple):
            args += [query_weight] * len(weights) + [kv_weight] * len(weights)
            specs += [own(at, size, TILE, True) for at, size in weights]
            specs += [own(at, size, kv_width, False) for at, size in weights]
            shape.append((tuple(len(p) for p in pieces), tuple(weights)))
        else:
            args += list(weights)
            specs += [pl.BlockSpec((w.shape[0], TILE), lambda j, sp: (0, j)) for w in weights]
            shape.append((tuple(len(p) for p in pieces), "help"))
    rows = [scratch[chosen[0]].shape[0] for chosen in sums]
    out = pl.pallas_call(
        functools.partial(
            product_kernel, shape, sums, kinds, (tiles, kv_width), base is not None
        ),
        out_shape=[jax.ShapeDtypeStruct((m, width + kv_width), k) for m in rows for k in kinds],
        grid_spec=pltpu.PrefetchScalarGridSpec(
            num_scalar_prefetch=1,
            grid=(tiles + 1,),
            in_specs=specs,
            out_specs=[pl.BlockSpec((m, TILE), lambda j, sp: (0, j)) for m in rows for _ in kinds],
            scratch_shapes=scratch,
        ),
        compiler_params=pltpu.CompilerParams(vmem_limit_bytes=48 * 2**20),
        cost_estimate=pl.CostEstimate(flops=10**10, bytes_accessed=10**6, transcendentals=0),
    )(sp, *args)
    out = [tuple(out[i : i + len(kinds)]) for i in range(0, len(out), len(kinds))]
    return out[0] if len(out) == 1 else out


def staged(tokens, query_weight, kv_weight):
    rows, depth = tokens.shape
    width = query_weight.shape[1]
    columns = width + kv_weight.shape[1]
    hid = lax.axis_index("hid")
    chip, core = hid // 2, hid % 2
    sp = jnp.zeros(1, jnp.int32)

    def at(x, i):
        return lax.dynamic_index_in_dim(x, i, keepdims=False)

    def shared_rows(parts):
        mine = gathered(jnp.concatenate([x[:, width:] for x in parts], 0))
        other = other_core(mine)
        return jnp.where(core == 0, mine, other), jnp.where(core == 0, other, mine)

    blocks, first = [], 0
    for sixteenths in SHARES:
        m = rows * sixteenths // 16
        blocks.append(lax.all_gather(tokens[first : first + m], "ffn", axis=0, tiled=True))
        first += m
    parts, early = [], None
    for block in blocks:
        if parts:
            block, _ = lax.optimization_barrier((block, parts[-1]))
        if len(parts) == len(SHARES) - 1:
            early = shared_rows(parts)
            block, early = lax.optimization_barrier((block, early))
        m = block.shape[0] // 4
        summed, sent = product(
            sp, query_weight, kv_weight, [([(block,)], ((0, depth),))], ((0,),)
        )
        summed = jnp.swapaxes(summed.reshape(2, 2, m, columns), 0, 1)
        sent = jnp.swapaxes(sent.reshape(2, 2, m, columns), 0, 1)
        summed = at(summed, core) + other_core(at(sent, 1 - core)).astype(F32)
        summed = at(summed, chip) + other_chip(at(summed, 1 - chip).astype(BF16)).astype(F32)
        parts.append(summed.astype(BF16))
    queries = jnp.concatenate([x[:, :width] for x in parts], 0)
    late = shared_rows(parts[-1:])
    shared = jnp.concatenate([early[0], late[0], early[1], late[1]], 0)
    return attention(core, queries, shared)


def solution(mesh):
    fits = mesh.shape["ffn"] == 4 and mesh.shape["hid"] == 4 and mesh.shape["grp"] == 2
    return jax.shard_map(
        staged if fits else general,
        mesh=mesh,
        in_specs=(P(("grp", "ffn"), "hid"), P("hid", "ffn"), P("hid", "ffn")),
        out_specs=P(("grp", "hid"), "ffn"),
        check_vma=False,
    )
```

```python
import functools

import jax
import jax.numpy as jnp
from jax import lax
from jax.experimental import pallas as pl
from jax.experimental.pallas import tpu as pltpu
from jax.sharding import PartitionSpec as P

HEAD_DIM = 256
SEQ = 1024
F32, BF16 = jnp.float32, jnp.bfloat16


def general(tokens, query_weight, kv_weight):
    local_rows = tokens.shape[0]
    total_rows = local_rows * lax.axis_size("ffn")
    query_count = total_rows // lax.axis_size("hid")
    heads_here = query_weight.shape[1] // HEAD_DIM
    kv_block = lax.all_gather(kv_weight, "ffn", axis=1, tiled=True)
    kv_partial = jnp.dot(tokens, kv_block, preferred_element_type=jnp.float32)
    kv_summed = lax.psum(kv_partial, "hid")
    shared = lax.all_gather(kv_summed.astype(jnp.bfloat16), "ffn", axis=0, tiled=True)
    keys = shared[:, :HEAD_DIM]
    values = shared[:, HEAD_DIM:]
    query_partial = jnp.dot(
        lax.all_gather(tokens, "ffn", axis=0, tiled=True),
        query_weight,
        preferred_element_type=jnp.float32,
    )
    query_summed = lax.psum_scatter(query_partial, "hid", scatter_dimension=0, tiled=True)
    queries = query_summed.astype(jnp.bfloat16)
    first_row = lax.axis_index("hid") * query_count
    query_pos = first_row + jnp.arange(query_count, dtype=jnp.int32)
    key_pos = jnp.arange(total_rows, dtype=jnp.int32)
    same_prompt = query_pos[:, None] // SEQ == key_pos[None, :] // SEQ
    visible = same_prompt & (key_pos[None, :] <= query_pos[:, None])
    scale = HEAD_DIM ** (-0.5)
    split_heads = queries.reshape(query_count, heads_here, HEAD_DIM)
    scores = (
        jnp.einsum("qhd,kd->hqk", split_heads, keys, preferred_element_type=jnp.float32) * scale
    )
    weights = jnp.where(visible[None, :, :], jnp.exp(scores), jnp.float32(0.0))
    probs = (weights / jnp.sum(weights, axis=2, keepdims=True)).astype(jnp.bfloat16)
    mixed = jnp.einsum("hqk,kd->qhd", probs, values, preferred_element_type=jnp.float32)
    return mixed.reshape(query_count, heads_here * HEAD_DIM).astype(jnp.bfloat16)


def attention_kernel(rows, where_ref, q_ref, kv_ref, o_ref):
    tile = rows // 2
    later = where_ref[0]
    scale = HEAD_DIM ** (-0.5) * 1.4426950408889634
    row = lax.broadcasted_iota(jnp.int32, (tile, tile), 0)
    col = lax.broadcasted_iota(jnp.int32, (tile, tile), 1)
    seen = col <= row

    def strip(first, count):
        q = q_ref[pl.ds(first * tile, tile), :]
        keys = kv_ref[: count * tile, :HEAD_DIM]
        values = kv_ref[: count * tile, HEAD_DIM:]
        s = lax.dot_general(q, keys, (((1,), (1,)), ((), ())), preferred_element_type=F32)
        last = jnp.where(seen, s[:, (count - 1) * tile :], -jnp.inf)
        s = last if count == 1 else jnp.concatenate([s[:, : (count - 1) * tile], last], axis=1)
        top = jnp.max(s, axis=1, keepdims=True)
        w = jnp.exp2((s - top) * scale)
        total = jnp.sum(w, axis=1, keepdims=True)
        mixed = jnp.dot(w.astype(BF16), values, preferred_element_type=F32)
        o_ref[pl.ds(first * tile, tile), :] = (mixed / total).astype(BF16)

    @pl.when(later == 0)
    def _():
        strip(0, 1)
        strip(1, 2)

    @pl.when(later == 1)
    def _():
        strip(0, 3)
        strip(1, 4)


def attention(later, queries, shared):
    rows, width = queries.shape
    return pl.pallas_call(
        functools.partial(attention_kernel, rows),
        out_shape=jax.ShapeDtypeStruct(queries.shape, BF16),
        grid_spec=pltpu.PrefetchScalarGridSpec(
            num_scalar_prefetch=1,
            grid=(width // HEAD_DIM,),
            in_specs=[
                pl.BlockSpec((rows, HEAD_DIM), lambda i, _: (0, i)),
                pl.BlockSpec(shared.shape, lambda i, _: (0, 0)),
            ],
            out_specs=pl.BlockSpec((rows, HEAD_DIM), lambda i, _: (0, i)),
        ),
        compiler_params=pltpu.CompilerParams(vmem_limit_bytes=32 * 2**20),
        cost_estimate=pl.CostEstimate(flops=6 * 10**9, bytes_accessed=5 * 10**6, transcendentals=3 * 10**6),
    )(later.reshape(1).astype(jnp.int32), queries, shared)


MID = [(1, 2), (2, 1)]
INTO = [(0, 1), (3, 2)]
OUT = [(1, 0), (2, 3)]
ORDER = ((0, 1, 2, 3), (1, 2, 1, 2), (2, 0, 3, 1), (3, 3, 0, 0))


def along(axis, pairs):
    return lambda x: lax.ppermute(x, axis, pairs)


def gate(xs, deps):
    deps = tuple(x for x in deps if x is not None)
    return lax.optimization_barrier((tuple(xs), deps))[0]


class Steps:
    def __init__(self):
        self.last, self.at, self.due = None, 0, {}

    def step(self):
        self.at += 1

    def start(self, move, x, due=1):
        (x,) = gate((x,), (self.last,))
        y = move(x)
        self.due.setdefault(self.at + due, []).append(y)
        return y

    def run(self, work, *xs, after=()):
        arrived = [y for at in list(self.due) if at <= self.at for y in self.due.pop(at)]
        xs = gate(xs, [self.last, *arrived, *after])
        out = work(*xs)
        self.last = jax.tree.leaves(out)[0]
        return out


def other_core(x):
    return lax.ppermute(x, "hid", [(i, i ^ 1) for i in range(4)])


def other_chip(x):
    return lax.ppermute(x, "hid", [(i, i ^ 2) for i in range(4)])


def gathered(x):
    z = lax.axis_index("ffn")
    got = [x] + [lax.ppermute(x, "ffn", [(i, i ^ k) for i in range(4)]) for k in (1, 2, 3)]
    columns = []
    for i in range(4):
        column = got[0]
        for k in (1, 2, 3):
            column = jnp.where((z ^ i) == k, got[k], column)
        columns.append(column)
    return jnp.concatenate(columns, 1)


TILE = 512


def product_kernel(terms, sums, kinds, heads, based, sp_ref, *refs):
    refs = list(refs)
    base = refs.pop(0) if based else None
    loaded = []
    for pieces, weights in terms:
        xs = [[refs.pop(0) for _ in range(n)] for n in pieces]
        if isinstance(weights, int):
            ws = [refs.pop(0) for _ in range(weights)]
            loaded.append((xs, ws, None))
        else:
            ws = [refs.pop(0) for _ in weights]
            loaded.append((xs, ws, [refs.pop(0) for _ in weights]))
    outs = [[refs.pop(0) for _ in kinds] for _ in sums]
    kept = refs
    j = pl.program_id(0)
    inner = sp_ref[0] == 1

    @pl.when(j == 0)
    def _():
        for (xs, _, _), keep in zip(loaded, kept):
            if len(xs) == 1 and len(xs[0]) == 1:
                continue
            at = 0
            for piece in xs:
                m = piece[0].shape[0]
                x = piece[0][...]
                if len(piece) == 2:
                    x = jnp.where(inner, x, piece[1][...])
                keep[pl.ds(at, m), :] = x
                at += m

    def total(chosen, part):
        acc = None
        if base is not None:
            acc = base[...] if part == "heads" else base[:, : heads[1]]
        for i in chosen:
            xs, ws, kvs = loaded[i]
            source = xs[0][0] if len(xs) == 1 and len(xs[0]) == 1 else kept[i]
            at = 0
            for k, w in enumerate(ws):
                if part == "heads":
                    w = w[...]
                else:
                    w = w[:, : heads[1]] if kvs is None else kvs[k][...]
                x = source[:, at : at + w.shape[0]]
                at += w.shape[0]
                y = jnp.dot(x, w, preferred_element_type=F32)
                acc = y if acc is None else acc + y
        return acc

    @pl.when(j < heads[0])
    def _():
        for chosen, out in zip(sums, outs):
            acc = total(chosen, "heads")
            for o in out:
                o[...] = acc.astype(o.dtype)

    @pl.when(j == heads[0])
    def _():
        for chosen, out in zip(sums, outs):
            acc = total(chosen, "kv")
            for o in out:
                o[:, : heads[1]] = acc.astype(o.dtype)


def product(sp, query_weight, kv_weight, terms, sums, kinds=(F32, BF16), base=None, base_at=0):
    width, kv_width = query_weight.shape[1], kv_weight.shape[1]
    tiles = width // TILE
    args, specs, shape, scratch = [], [], [], []

    def own(at, size, columns, which):
        def index(j, sp):
            return (at if isinstance(at, int) else pl.multiple_of(sp[at[0]], 128), jnp.minimum(j, tiles - 1) * TILE if which else 0)

        return pl.BlockSpec((pl.Element(size), pl.Element(columns)), index)

    if base is not None:
        m = sum(piece[0].shape[0] for piece in terms[0][0])
        args.append(base)
        specs.append(pl.BlockSpec((m, TILE), lambda j, sp: (base_at, j)))
    for pieces, weights in terms:
        for piece in pieces:
            for x in piece:
                args.append(x)
                specs.append(pl.BlockSpec(x.shape, lambda j, sp: (0, 0)))
        rows = sum(piece[0].shape[0] for piece in pieces)
        depth = pieces[0][0].shape[1]
        scratch.append(pltpu.VMEM((rows, depth), BF16))
        if isinstance(weights[0], tuple):
            args += [query_weight] * len(weights) + [kv_weight] * len(weights)
            specs += [own(at, size, TILE, True) for at, size in weights]
            specs += [own(at, size, kv_width, False) for at, size in weights]
            shape.append((tuple(len(p) for p in pieces), tuple(weights)))
        else:
            args += list(weights)
            specs += [pl.BlockSpec((w.shape[0], TILE), lambda j, sp: (0, j)) for w in weights]
            shape.append((tuple(len(p) for p in pieces), len(weights)))
    rows = [scratch[chosen[0]].shape[0] for chosen in sums]
    out = pl.pallas_call(
        functools.partial(
            product_kernel, shape, sums, kinds, (tiles, kv_width), base is not None
        ),
        out_shape=[jax.ShapeDtypeStruct((m, width + kv_width), k) for m in rows for k in kinds],
        grid_spec=pltpu.PrefetchScalarGridSpec(
            num_scalar_prefetch=1,
            grid=(tiles + 1,),
            in_specs=specs,
            out_specs=[pl.BlockSpec((m, TILE), lambda j, sp: (0, j)) for m in rows for _ in kinds],
            scratch_shapes=scratch,
        ),
        compiler_params=pltpu.CompilerParams(vmem_limit_bytes=60 * 2**20),
        cost_estimate=pl.CostEstimate(flops=10**10, bytes_accessed=10**6, transcendentals=0),
    )(sp, *args)
    out = [tuple(out[i : i + len(kinds)]) for i in range(0, len(out), len(kinds))]
    return out[0] if len(out) == 1 else out


def staged(tokens, query_weight, kv_weight):
    rows, depth = tokens.shape
    width = query_weight.shape[1]
    columns = width + kv_weight.shape[1]
    z, hid, grp = (lax.axis_index(name) for name in ("ffn", "hid", "grp"))
    chip, core = hid // 2, hid % 2
    part = depth // 6 // 128 * 128
    first = depth - 2 * part
    mid, into, out = along("ffn", MID), along("ffn", INTO), along("ffn", OUT)
    across = along("grp", [(0, 1), (1, 0)])
    own_at, far_at = first + grp * part, first + (1 - grp) * part
    inner = (z == 1) | (z == 2)
    sp = jnp.stack([inner, own_at, far_at]).astype(jnp.int32)
    weights1 = ((0, first),)
    weights2 = (((1,), part), ((2,), part))
    early_rows = rows // 2
    spans = ((0, early_rows), (early_rows, rows - early_rows))
    share = part // 2

    def at(x, i):
        return lax.dynamic_index_in_dim(x, i, keepdims=False)

    def from_plane(x, block):
        stage = 0
        for i, order in enumerate(ORDER):
            stage += i * (sum(jnp.where(z == k, b, 0) for k, b in enumerate(order)) == block)
        m = x.shape[0] // 4
        return lax.dynamic_slice_in_dim(x, stage * m, m, 0)

    def give_core(x):
        return jnp.stack([from_plane(x, 2 * i + 1 - core) for i in range(2)])

    def over_cores(x, got):
        keep = from_plane(x, hid) + at(got, chip).astype(F32)
        give = from_plane(x, hid ^ 2) + at(got, 1 - chip).astype(F32)
        return keep, give.astype(BF16)

    def shared_rows(parts):
        mine = gathered(jnp.concatenate([x[:, width:] for x in parts], 0))
        other = other_core(mine)
        return jnp.where(core == 0, mine, other), jnp.where(core == 0, other, mine)

    def mark(*xs):
        return sum(x[:16, :128] for x in xs)

    def weights_at(i):
        return jnp.concatenate(
            [
                lax.dynamic_slice_in_dim(w, own_at + i * share, share, 0)
                for w in (query_weight, kv_weight)
            ],
            1,
        )

    def shares(rest, w):
        return product(
            sp,
            query_weight,
            kv_weight,
            [([(x,) for x in rest], weights2), ([(x,) for x in rest], w)],
            ((0,), (1,)),
        )

    def whole(pieces, base):
        return product(
            sp, query_weight, kv_weight, [(pieces, weights1)], ((0,),), base=base
        )

    t1 = [tokens[a : a + m, :first] for a, m in spans]
    t2 = [
        jnp.concatenate(
            [lax.dynamic_slice(tokens, (a, i), (m, part)) for i in (own_at, far_at)], 1
        )
        for a, m in spans
    ]
    s = Steps()
    c2 = [s.start(into, x) for x in t2]
    b1 = [s.start(mid, t1[0])]
    e1 = [s.start(out, t1[0])]
    s.step()
    s.run(mark, c2[0], b1[0])
    w_in = [s.start(into, weights_at(0))]
    d2 = [s.start(mid, x) for x in c2]
    e1.append(s.start(out, t1[1]))
    s.step()
    s.run(mark, w_in[0], d2[0])
    w_in.append(s.start(into, weights_at(1)))
    b1.append(s.start(mid, t1[1]))
    f1 = [s.start(out, b1[0])]
    w_far = [s.start(across, w_in[0])]
    s.step()
    s.run(mark, w_in[1], b1[1])
    c1 = [s.start(into, t1[0])]
    b2 = [s.start(mid, x) for x in t2]
    f1.append(s.start(out, b1[1]))
    w_far.append(s.start(across, w_in[1]))
    s.step()
    s.run(mark, c1[0], b2[0])
    c1.append(s.start(into, t1[1]))
    d1 = [s.start(mid, c1[0])]
    rest = [[jnp.where(inner, x, jnp.zeros_like(x)), *y] for x, *y in zip(t2, b2, c2, d2)]
    w_help = w_in + w_far

    def complete(x, y):
        return (x + y.astype(F32)).astype(BF16)

    def finished(q, got, o):
        return (q + got.astype(F32) + o.astype(F32)).astype(BF16)

    def block(i, after=None):
        b, e, c, f, d, g = gate([y[i] for y in (b1, e1, c1, f1, d1, g1)], (after,))
        return [(t1[i],), (b, e), (c, f), (d, g)]

    (p0, _), (h0, h0_16) = s.run(shares, rest[0], w_help)
    s.step()
    s.run(mark, c1[1], d1[0])
    d1.append(s.start(mid, c1[1]))
    g1 = [s.start(out, d1[0])]
    (h0_16,) = gate((h0_16,), (s.last,))
    h0_core = s.start(other_core, give_core(h0_16))
    h0, h0_give = s.run(over_cores, h0, h0_core)
    h0_got = s.start(other_chip, h0_give)
    (p1, _), (h1, h1_16) = s.run(shares, rest[1], w_help)
    s.step()
    h0 = s.run(complete, h0, h0_got)
    g1.append(s.start(out, d1[1]))
    o0 = s.start(out, h0, 2)
    (h1_16,) = gate((h1_16,), (s.last,))
    h1_core = s.start(other_core, give_core(h1_16))
    h1, h1_give = s.run(over_cores, h1, h1_core)
    h1_got = s.start(other_chip, h1_give)
    q0, q0_16 = s.run(whole, block(0, h1_give), p0)
    s.step()
    h1 = s.run(complete, h1, h1_got)
    o1 = s.start(out, h1, 9)
    q0_core = s.start(other_core, give_core(q0_16))
    q0, q0_give = s.run(over_cores, q0, q0_core)
    q0_got = s.start(other_chip, q0_give)
    q1, q1_16 = s.run(whole, block(1, q0_give), p1)
    s.step()
    q0 = s.run(finished, q0, q0_got, o0)
    q1_core = s.start(other_core, give_core(q1_16))
    q1, q1_give = s.run(over_cores, q1, q1_core)
    q1_got = other_chip(q1_give)
    early = shared_rows([q0])
    q1 = finished(q1, q1_got, o1)
    queries = jnp.concatenate([x[:, :width] for x in (q0, q1)], 0)
    late = shared_rows([q1])
    shared = jnp.concatenate([early[0], late[0], early[1], late[1]], 0)
    return attention(core, queries, shared)


def solution(mesh):
    fits = mesh.shape["ffn"] == 4 and mesh.shape["hid"] == 4 and mesh.shape["grp"] == 2
    return jax.shard_map(
        staged if fits else general,
        mesh=mesh,
        in_specs=(P(("grp", "ffn"), "hid"), P("hid", "ffn"), P("hid", "ffn")),
        out_specs=P(("grp", "hid"), "ffn"),
        check_vma=False,
    )
```

```python
import functools

import jax
import jax.numpy as jnp
from jax import lax
from jax.experimental import pallas as pl
from jax.experimental.pallas import tpu as pltpu
from jax.sharding import PartitionSpec as P

HEAD_DIM = 256
SEQ = 1024
F32, BF16 = jnp.float32, jnp.bfloat16


def general(tokens, query_weight, kv_weight):
    local_rows = tokens.shape[0]
    total_rows = local_rows * lax.axis_size("ffn")
    query_count = total_rows // lax.axis_size("hid")
    heads_here = query_weight.shape[1] // HEAD_DIM
    kv_block = lax.all_gather(kv_weight, "ffn", axis=1, tiled=True)
    kv_partial = jnp.dot(tokens, kv_block, preferred_element_type=jnp.float32)
    kv_summed = lax.psum(kv_partial, "hid")
    shared = lax.all_gather(kv_summed.astype(jnp.bfloat16), "ffn", axis=0, tiled=True)
    keys = shared[:, :HEAD_DIM]
    values = shared[:, HEAD_DIM:]
    query_partial = jnp.dot(
        lax.all_gather(tokens, "ffn", axis=0, tiled=True),
        query_weight,
        preferred_element_type=jnp.float32,
    )
    query_summed = lax.psum_scatter(query_partial, "hid", scatter_dimension=0, tiled=True)
    queries = query_summed.astype(jnp.bfloat16)
    first_row = lax.axis_index("hid") * query_count
    query_pos = first_row + jnp.arange(query_count, dtype=jnp.int32)
    key_pos = jnp.arange(total_rows, dtype=jnp.int32)
    same_prompt = query_pos[:, None] // SEQ == key_pos[None, :] // SEQ
    visible = same_prompt & (key_pos[None, :] <= query_pos[:, None])
    scale = HEAD_DIM ** (-0.5)
    split_heads = queries.reshape(query_count, heads_here, HEAD_DIM)
    scores = (
        jnp.einsum("qhd,kd->hqk", split_heads, keys, preferred_element_type=jnp.float32) * scale
    )
    weights = jnp.where(visible[None, :, :], jnp.exp(scores), jnp.float32(0.0))
    probs = (weights / jnp.sum(weights, axis=2, keepdims=True)).astype(jnp.bfloat16)
    mixed = jnp.einsum("hqk,kd->qhd", probs, values, preferred_element_type=jnp.float32)
    return mixed.reshape(query_count, heads_here * HEAD_DIM).astype(jnp.bfloat16)


def attention_kernel(rows, where_ref, q_ref, kv_ref, o_ref):
    tile = rows // 2
    later = where_ref[0]
    scale = HEAD_DIM ** (-0.5) * 1.4426950408889634
    row = lax.broadcasted_iota(jnp.int32, (tile, tile), 0)
    col = lax.broadcasted_iota(jnp.int32, (tile, tile), 1)
    seen = col <= row

    def strip(first, count):
        q = q_ref[pl.ds(first * tile, tile), :]
        keys = kv_ref[: count * tile, :HEAD_DIM]
        values = kv_ref[: count * tile, HEAD_DIM:]
        s = lax.dot_general(q, keys, (((1,), (1,)), ((), ())), preferred_element_type=F32)
        last = jnp.where(seen, s[:, (count - 1) * tile :], -jnp.inf)
        s = last if count == 1 else jnp.concatenate([s[:, : (count - 1) * tile], last], axis=1)
        top = jnp.max(s, axis=1, keepdims=True)
        w = jnp.exp2((s - top) * scale)
        total = jnp.sum(w, axis=1, keepdims=True)
        mixed = jnp.dot(w.astype(BF16), values, preferred_element_type=F32)
        o_ref[pl.ds(first * tile, tile), :] = (mixed / total).astype(BF16)

    @pl.when(later == 0)
    def _():
        strip(0, 1)
        strip(1, 2)

    @pl.when(later == 1)
    def _():
        strip(0, 3)
        strip(1, 4)


def attention(later, queries, shared):
    rows, width = queries.shape
    return pl.pallas_call(
        functools.partial(attention_kernel, rows),
        out_shape=jax.ShapeDtypeStruct(queries.shape, BF16),
        grid_spec=pltpu.PrefetchScalarGridSpec(
            num_scalar_prefetch=1,
            grid=(width // HEAD_DIM,),
            in_specs=[
                pl.BlockSpec((rows, HEAD_DIM), lambda i, _: (0, i)),
                pl.BlockSpec(shared.shape, lambda i, _: (0, 0)),
            ],
            out_specs=pl.BlockSpec((rows, HEAD_DIM), lambda i, _: (0, i)),
        ),
        compiler_params=pltpu.CompilerParams(vmem_limit_bytes=32 * 2**20),
        cost_estimate=pl.CostEstimate(flops=6 * 10**9, bytes_accessed=5 * 10**6, transcendentals=3 * 10**6),
    )(later.reshape(1).astype(jnp.int32), queries, shared)


MID = [(1, 2), (2, 1)]
INTO = [(0, 1), (3, 2)]
OUT = [(1, 0), (2, 3)]
ORDER = ((0, 1, 2, 3), (1, 2, 1, 2), (2, 0, 3, 1), (3, 3, 0, 0))


def along(axis, pairs):
    return lambda x: lax.ppermute(x, axis, pairs)


def gate(xs, deps):
    deps = tuple(x for x in deps if x is not None)
    return lax.optimization_barrier((tuple(xs), deps))[0]


class Steps:
    def __init__(self):
        self.last, self.at, self.due = None, 0, {}

    def step(self):
        self.at += 1

    def start(self, move, x, due=1):
        (x,) = gate((x,), (self.last,))
        y = move(x)
        self.due.setdefault(self.at + due, []).append(y)
        return y

    def run(self, work, *xs, after=()):
        arrived = [y for at in list(self.due) if at <= self.at for y in self.due.pop(at)]
        xs = gate(xs, [self.last, *arrived, *after])
        out = work(*xs)
        self.last = jax.tree.leaves(out)[0]
        return out


def other_core(x):
    return lax.ppermute(x, "hid", [(i, i ^ 1) for i in range(4)])


def other_chip(x):
    return lax.ppermute(x, "hid", [(i, i ^ 2) for i in range(4)])


def gathered(x):
    z = lax.axis_index("ffn")
    got = [x] + [lax.ppermute(x, "ffn", [(i, i ^ k) for i in range(4)]) for k in (1, 2, 3)]
    columns = []
    for i in range(4):
        column = got[0]
        for k in (1, 2, 3):
            column = jnp.where((z ^ i) == k, got[k], column)
        columns.append(column)
    return jnp.concatenate(columns, 1)


TILE = 512


def product_kernel(terms, sums, kinds, heads, based, sp_ref, *refs):
    refs = list(refs)
    base = refs.pop(0) if based else None
    loaded = []
    for pieces, weights in terms:
        xs = [[refs.pop(0) for _ in range(n)] for n in pieces]
        if isinstance(weights, int):
            ws = [refs.pop(0) for _ in range(weights)]
            loaded.append((xs, ws, None))
        else:
            ws = [refs.pop(0) for _ in weights]
            loaded.append((xs, ws, [refs.pop(0) for _ in weights]))
    outs = [[refs.pop(0) for _ in kinds] for _ in sums]
    kept = refs
    j = pl.program_id(0)
    inner = sp_ref[0] == 1

    @pl.when(j == 0)
    def _():
        for (xs, _, _), keep in zip(loaded, kept):
            if len(xs) == 1 and len(xs[0]) == 1:
                continue
            at = 0
            for piece in xs:
                m = piece[0].shape[0]
                x = piece[0][...]
                if len(piece) == 2:
                    x = jnp.where(inner, x, piece[1][...])
                keep[pl.ds(at, m), :] = x
                at += m

    def total(chosen, part):
        acc = None
        if base is not None:
            acc = base[...] if part == "heads" else base[:, : heads[1]]
        for i in chosen:
            xs, ws, kvs = loaded[i]
            source = xs[0][0] if len(xs) == 1 and len(xs[0]) == 1 else kept[i]
            at = 0
            for k, w in enumerate(ws):
                if part == "heads":
                    w = w[...]
                else:
                    w = w[:, : heads[1]] if kvs is None else kvs[k][...]
                x = source[:, at : at + w.shape[0]]
                at += w.shape[0]
                y = jnp.dot(x, w, preferred_element_type=F32)
                acc = y if acc is None else acc + y
        return acc

    @pl.when(j < heads[0])
    def _():
        for chosen, out in zip(sums, outs):
            acc = total(chosen, "heads")
            for o in out:
                o[...] = acc.astype(o.dtype)

    @pl.when(j == heads[0])
    def _():
        for chosen, out in zip(sums, outs):
            acc = total(chosen, "kv")
            for o in out:
                o[:, : heads[1]] = acc.astype(o.dtype)


def product(sp, query_weight, kv_weight, terms, sums, kinds=(F32, BF16), base=None, base_at=0):
    width, kv_width = query_weight.shape[1], kv_weight.shape[1]
    tiles = width // TILE
    args, specs, shape, scratch = [], [], [], []

    def own(at, size, columns, which):
        def index(j, sp):
            return (at if isinstance(at, int) else pl.multiple_of(sp[at[0]], 128), jnp.minimum(j, tiles - 1) * TILE if which else 0)

        return pl.BlockSpec((pl.Element(size), pl.Element(columns)), index)

    if base is not None:
        m = sum(piece[0].shape[0] for piece in terms[0][0])
        args.append(base)
        specs.append(pl.BlockSpec((m, TILE), lambda j, sp: (base_at, j)))
    for pieces, weights in terms:
        for piece in pieces:
            for x in piece:
                args.append(x)
                specs.append(pl.BlockSpec(x.shape, lambda j, sp: (0, 0)))
        rows = sum(piece[0].shape[0] for piece in pieces)
        depth = pieces[0][0].shape[1]
        scratch.append(pltpu.VMEM((rows, depth), BF16))
        if isinstance(weights[0], tuple):
            args += [query_weight] * len(weights) + [kv_weight] * len(weights)
            specs += [own(at, size, TILE, True) for at, size in weights]
            specs += [own(at, size, kv_width, False) for at, size in weights]
            shape.append((tuple(len(p) for p in pieces), tuple(weights)))
        else:
            args += list(weights)
            specs += [pl.BlockSpec((w.shape[0], TILE), lambda j, sp: (0, j)) for w in weights]
            shape.append((tuple(len(p) for p in pieces), len(weights)))
    rows = [scratch[chosen[0]].shape[0] for chosen in sums]
    out = pl.pallas_call(
        functools.partial(
            product_kernel, shape, sums, kinds, (tiles, kv_width), base is not None
        ),
        out_shape=[jax.ShapeDtypeStruct((m, width + kv_width), k) for m in rows for k in kinds],
        grid_spec=pltpu.PrefetchScalarGridSpec(
            num_scalar_prefetch=1,
            grid=(tiles + 1,),
            in_specs=specs,
            out_specs=[pl.BlockSpec((m, TILE), lambda j, sp: (0, j)) for m in rows for _ in kinds],
            scratch_shapes=scratch,
        ),
        compiler_params=pltpu.CompilerParams(vmem_limit_bytes=60 * 2**20),
        cost_estimate=pl.CostEstimate(flops=10**10, bytes_accessed=10**6, transcendentals=0),
    )(sp, *args)
    out = [tuple(out[i : i + len(kinds)]) for i in range(0, len(out), len(kinds))]
    return out[0] if len(out) == 1 else out


def staged(tokens, query_weight, kv_weight):
    rows, depth = tokens.shape
    width = query_weight.shape[1]
    columns = width + kv_weight.shape[1]
    z, hid, grp = (lax.axis_index(name) for name in ("ffn", "hid", "grp"))
    chip, core = hid // 2, hid % 2
    part = depth // 6 // 128 * 128
    first = depth - 2 * part
    mid, into, out = along("ffn", MID), along("ffn", INTO), along("ffn", OUT)
    across = along("grp", [(0, 1), (1, 0)])
    own_at, far_at = first + grp * part, first + (1 - grp) * part
    inner = (z == 1) | (z == 2)
    sp = jnp.stack([inner, own_at, far_at]).astype(jnp.int32)
    weights1 = ((0, first),)
    weights2 = (((1,), part), ((2,), part))
    early_rows = rows * 15 // 32
    spans = ((0, early_rows), (early_rows, rows - early_rows))
    share = part // 2

    def at(x, i):
        return lax.dynamic_index_in_dim(x, i, keepdims=False)

    def from_plane(x, block):
        stage = 0
        for i, order in enumerate(ORDER):
            stage += i * (sum(jnp.where(z == k, b, 0) for k, b in enumerate(order)) == block)
        m = x.shape[0] // 4
        return lax.dynamic_slice_in_dim(x, stage * m, m, 0)

    def give_core(x):
        return jnp.stack([from_plane(x, 2 * i + 1 - core) for i in range(2)])

    def over_cores(x, got):
        keep = from_plane(x, hid) + at(got, chip).astype(F32)
        give = from_plane(x, hid ^ 2) + at(got, 1 - chip).astype(F32)
        return keep, give.astype(BF16)

    def shared_rows(parts):
        mine = gathered(jnp.concatenate([x[:, width:] for x in parts], 0))
        other = other_core(mine)
        return jnp.where(core == 0, mine, other), jnp.where(core == 0, other, mine)

    def mark(*xs):
        return sum(x[:16, :128] for x in xs)

    def weights_at(i):
        return jnp.concatenate(
            [
                lax.dynamic_slice_in_dim(w, own_at + i * share, share, 0)
                for w in (query_weight, kv_weight)
            ],
            1,
        )

    def shares(rest, w):
        return product(
            sp,
            query_weight,
            kv_weight,
            [([(x,) for x in rest], weights2), ([(x,) for x in rest], w)],
            ((0,), (1,)),
        )

    def whole(pieces, base):
        return product(
            sp, query_weight, kv_weight, [(pieces, weights1)], ((0,),), base=base
        )

    t1 = [tokens[a : a + m, :first] for a, m in spans]
    t2 = [
        jnp.concatenate(
            [lax.dynamic_slice(tokens, (a, i), (m, part)) for i in (own_at, far_at)], 1
        )
        for a, m in spans
    ]
    s = Steps()
    c2 = [s.start(into, x) for x in t2]
    b1 = [s.start(mid, t1[0])]
    e1 = [s.start(out, t1[0])]
    s.step()
    s.run(mark, c2[0], b1[0])
    w_in = [s.start(into, weights_at(0))]
    d2 = [s.start(mid, x) for x in c2]
    e1.append(s.start(out, t1[1]))
    s.step()
    s.run(mark, w_in[0], d2[0])
    w_in.append(s.start(into, weights_at(1)))
    b1.append(s.start(mid, t1[1]))
    f1 = [s.start(out, b1[0])]
    w_far = [s.start(across, w_in[0])]
    s.step()
    s.run(mark, w_in[1], b1[1])
    c1 = [s.start(into, t1[0])]
    b2 = [s.start(mid, x) for x in t2]
    f1.append(s.start(out, b1[1]))
    w_far.append(s.start(across, w_in[1]))
    s.step()
    s.run(mark, c1[0], b2[0])
    c1.append(s.start(into, t1[1]))
    d1 = [s.start(mid, c1[0])]
    rest = [[jnp.where(inner, x, jnp.zeros_like(x)), *y] for x, *y in zip(t2, b2, c2, d2)]
    w_help = w_in + w_far

    def complete(x, y):
        return (x + y.astype(F32)).astype(BF16)

    def finished(q, got, o):
        return (q + got.astype(F32) + o.astype(F32)).astype(BF16)

    def block(i, after=None):
        b, e, c, f, d, g = gate([y[i] for y in (b1, e1, c1, f1, d1, g1)], (after,))
        return [(t1[i],), (b, e), (c, f), (d, g)]

    (p0, _), (h0, h0_16) = s.run(shares, rest[0], w_help)
    s.step()
    s.run(mark, c1[1], d1[0])
    d1.append(s.start(mid, c1[1]))
    g1 = [s.start(out, d1[0])]
    (h0_16,) = gate((h0_16,), (s.last,))
    h0_core = s.start(other_core, give_core(h0_16))
    h0, h0_give = s.run(over_cores, h0, h0_core)
    h0_got = s.start(other_chip, h0_give)
    (p1, _), (h1, h1_16) = s.run(shares, rest[1], w_help)
    s.step()
    h0 = s.run(complete, h0, h0_got)
    g1.append(s.start(out, d1[1]))
    o0 = s.start(out, h0, 2)
    (h1_16,) = gate((h1_16,), (s.last,))
    h1_core = s.start(other_core, give_core(h1_16))
    h1, h1_give = s.run(over_cores, h1, h1_core)
    h1_got = s.start(other_chip, h1_give)
    q0, q0_16 = s.run(whole, block(0, h1_give), p0)
    s.step()
    h1 = s.run(complete, h1, h1_got)
    o1 = s.start(out, h1, 9)
    q0_core = s.start(other_core, give_core(q0_16))
    q0, q0_give = s.run(over_cores, q0, q0_core)
    q0_got = s.start(other_chip, q0_give)
    q1, q1_16 = s.run(whole, block(1, q0_give), p1)
    s.step()
    q0 = s.run(finished, q0, q0_got, o0)
    q1_core = s.start(other_core, give_core(q1_16))
    q1, q1_give = s.run(over_cores, q1, q1_core)
    q1_got = other_chip(q1_give)
    early = shared_rows([q0])
    q1 = finished(q1, q1_got, o1)
    queries = jnp.concatenate([x[:, :width] for x in (q0, q1)], 0)
    late = shared_rows([q1])
    shared = jnp.concatenate([early[0], late[0], early[1], late[1]], 0)
    return attention(core, queries, shared)


def solution(mesh):
    fits = mesh.shape["ffn"] == 4 and mesh.shape["hid"] == 4 and mesh.shape["grp"] == 2
    return jax.shard_map(
        staged if fits else general,
        mesh=mesh,
        in_specs=(P(("grp", "ffn"), "hid"), P("hid", "ffn"), P("hid", "ffn")),
        out_specs=P(("grp", "hid"), "ffn"),
        check_vma=False,
    )
```

```python
import functools

import jax
import jax.numpy as jnp
from jax import lax
from jax.experimental import pallas as pl
from jax.experimental.pallas import tpu as pltpu
from jax.sharding import PartitionSpec as P

HEAD_DIM = 256
SEQ = 1024
F32, BF16 = jnp.float32, jnp.bfloat16


def general(tokens, query_weight, kv_weight):
    local_rows = tokens.shape[0]
    total_rows = local_rows * lax.axis_size("ffn")
    query_count = total_rows // lax.axis_size("hid")
    heads_here = query_weight.shape[1] // HEAD_DIM
    kv_block = lax.all_gather(kv_weight, "ffn", axis=1, tiled=True)
    kv_partial = jnp.dot(tokens, kv_block, preferred_element_type=jnp.float32)
    kv_summed = lax.psum(kv_partial, "hid")
    shared = lax.all_gather(kv_summed.astype(jnp.bfloat16), "ffn", axis=0, tiled=True)
    keys = shared[:, :HEAD_DIM]
    values = shared[:, HEAD_DIM:]
    query_partial = jnp.dot(
        lax.all_gather(tokens, "ffn", axis=0, tiled=True),
        query_weight,
        preferred_element_type=jnp.float32,
    )
    query_summed = lax.psum_scatter(query_partial, "hid", scatter_dimension=0, tiled=True)
    queries = query_summed.astype(jnp.bfloat16)
    first_row = lax.axis_index("hid") * query_count
    query_pos = first_row + jnp.arange(query_count, dtype=jnp.int32)
    key_pos = jnp.arange(total_rows, dtype=jnp.int32)
    same_prompt = query_pos[:, None] // SEQ == key_pos[None, :] // SEQ
    visible = same_prompt & (key_pos[None, :] <= query_pos[:, None])
    scale = HEAD_DIM ** (-0.5)
    split_heads = queries.reshape(query_count, heads_here, HEAD_DIM)
    scores = (
        jnp.einsum("qhd,kd->hqk", split_heads, keys, preferred_element_type=jnp.float32) * scale
    )
    weights = jnp.where(visible[None, :, :], jnp.exp(scores), jnp.float32(0.0))
    probs = (weights / jnp.sum(weights, axis=2, keepdims=True)).astype(jnp.bfloat16)
    mixed = jnp.einsum("hqk,kd->qhd", probs, values, preferred_element_type=jnp.float32)
    return mixed.reshape(query_count, heads_here * HEAD_DIM).astype(jnp.bfloat16)


def attention_kernel(rows, where_ref, q_ref, kv_ref, o_ref):
    tile = rows // 2
    later = where_ref[0]
    scale = HEAD_DIM ** (-0.5) * 1.4426950408889634
    row = lax.broadcasted_iota(jnp.int32, (tile, tile), 0)
    col = lax.broadcasted_iota(jnp.int32, (tile, tile), 1)
    seen = col <= row

    def strip(first, count):
        q = q_ref[pl.ds(first * tile, tile), :]
        keys = kv_ref[: count * tile, :HEAD_DIM]
        values = kv_ref[: count * tile, HEAD_DIM:]
        s = lax.dot_general(q, keys, (((1,), (1,)), ((), ())), preferred_element_type=F32)
        last = jnp.where(seen, s[:, (count - 1) * tile :], -jnp.inf)
        s = last if count == 1 else jnp.concatenate([s[:, : (count - 1) * tile], last], axis=1)
        top = jnp.max(s, axis=1, keepdims=True)
        w = jnp.exp2((s - top) * scale)
        total = jnp.sum(w, axis=1, keepdims=True)
        mixed = jnp.dot(w.astype(BF16), values, preferred_element_type=F32)
        o_ref[pl.ds(first * tile, tile), :] = (mixed / total).astype(BF16)

    @pl.when(later == 0)
    def _():
        strip(0, 1)
        strip(1, 2)

    @pl.when(later == 1)
    def _():
        strip(0, 3)
        strip(1, 4)


def attention(later, queries, shared):
    rows, width = queries.shape
    return pl.pallas_call(
        functools.partial(attention_kernel, rows),
        out_shape=jax.ShapeDtypeStruct(queries.shape, BF16),
        grid_spec=pltpu.PrefetchScalarGridSpec(
            num_scalar_prefetch=1,
            grid=(width // HEAD_DIM,),
            in_specs=[
                pl.BlockSpec((rows, HEAD_DIM), lambda i, _: (0, i)),
                pl.BlockSpec(shared.shape, lambda i, _: (0, 0)),
            ],
            out_specs=pl.BlockSpec((rows, HEAD_DIM), lambda i, _: (0, i)),
        ),
        compiler_params=pltpu.CompilerParams(vmem_limit_bytes=32 * 2**20),
        cost_estimate=pl.CostEstimate(flops=6 * 10**9, bytes_accessed=5 * 10**6, transcendentals=3 * 10**6),
    )(later.reshape(1).astype(jnp.int32), queries, shared)


MID = [(1, 2), (2, 1)]
INTO = [(0, 1), (3, 2)]
OUT = [(1, 0), (2, 3)]
ORDER = ((0, 1, 2, 3), (1, 2, 1, 2), (2, 0, 3, 1), (3, 3, 0, 0))


def along(axis, pairs):
    return lambda x: lax.ppermute(x, axis, pairs)


def gate(xs, deps):
    deps = tuple(x for x in deps if x is not None)
    return lax.optimization_barrier((tuple(xs), deps))[0]


class Steps:
    def __init__(self):
        self.last, self.at, self.due = None, 0, {}

    def step(self):
        self.at += 1

    def start(self, move, x, due=1):
        (x,) = gate((x,), (self.last,))
        y = move(x)
        self.due.setdefault(self.at + due, []).append(y)
        return y

    def run(self, work, *xs, after=()):
        arrived = [y for at in list(self.due) if at <= self.at for y in self.due.pop(at)]
        xs = gate(xs, [self.last, *arrived, *after])
        out = work(*xs)
        self.last = jax.tree.leaves(out)[0]
        return out


def other_core(x):
    return lax.ppermute(x, "hid", [(i, i ^ 1) for i in range(4)])


def other_chip(x):
    return lax.ppermute(x, "hid", [(i, i ^ 2) for i in range(4)])


def gathered(x):
    z = lax.axis_index("ffn")
    got = [x] + [lax.ppermute(x, "ffn", [(i, i ^ k) for i in range(4)]) for k in (1, 2, 3)]
    columns = []
    for i in range(4):
        column = got[0]
        for k in (1, 2, 3):
            column = jnp.where((z ^ i) == k, got[k], column)
        columns.append(column)
    return jnp.concatenate(columns, 1)


TILE = 512


def product_kernel(terms, sums, kinds, heads, based, sp_ref, *refs):
    refs = list(refs)
    base = refs.pop(0) if based else None
    loaded = []
    for pieces, weights in terms:
        xs = [[refs.pop(0) for _ in range(n)] for n in pieces]
        if isinstance(weights, int):
            ws = [refs.pop(0) for _ in range(weights)]
            loaded.append((xs, ws, None))
        else:
            ws = [refs.pop(0) for _ in weights]
            loaded.append((xs, ws, [refs.pop(0) for _ in weights]))
    outs = [[refs.pop(0) for _ in kinds] for _ in sums]
    kept = refs
    j = pl.program_id(0)
    inner = sp_ref[0] == 1

    @pl.when(j == 0)
    def _():
        for (xs, _, _), keep in zip(loaded, kept):
            if len(xs) == 1 and len(xs[0]) == 1:
                continue
            at = 0
            for piece in xs:
                m = piece[0].shape[0]
                x = piece[0][...]
                if len(piece) == 2:
                    x = jnp.where(inner, x, piece[1][...])
                keep[pl.ds(at, m), :] = x
                at += m

    def total(chosen, part):
        acc = None
        if base is not None:
            acc = base[...] if part == "heads" else base[:, : heads[1]]
        for i in chosen:
            xs, ws, kvs = loaded[i]
            source = xs[0][0] if len(xs) == 1 and len(xs[0]) == 1 else kept[i]
            at = 0
            for k, w in enumerate(ws):
                if part == "heads":
                    w = w[...]
                else:
                    w = w[:, : heads[1]] if kvs is None else kvs[k][...]
                x = source[:, at : at + w.shape[0]]
                at += w.shape[0]
                y = jnp.dot(x, w, preferred_element_type=F32)
                acc = y if acc is None else acc + y
        return acc

    @pl.when(j < heads[0])
    def _():
        for chosen, out in zip(sums, outs):
            acc = total(chosen, "heads")
            for o in out:
                o[...] = acc.astype(o.dtype)

    @pl.when(j == heads[0])
    def _():
        for chosen, out in zip(sums, outs):
            acc = total(chosen, "kv")
            for o in out:
                o[:, : heads[1]] = acc.astype(o.dtype)


def product(sp, query_weight, kv_weight, terms, sums, kinds=(F32, BF16), base=None, base_at=0):
    width, kv_width = query_weight.shape[1], kv_weight.shape[1]
    tiles = width // TILE
    args, specs, shape, scratch = [], [], [], []

    def own(at, size, columns, which):
        def index(j, sp):
            return (at if isinstance(at, int) else pl.multiple_of(sp[at[0]], 128), jnp.minimum(j, tiles - 1) * TILE if which else 0)

        return pl.BlockSpec((pl.Element(size), pl.Element(columns)), index)

    if base is not None:
        m = sum(piece[0].shape[0] for piece in terms[0][0])
        args.append(base)
        specs.append(pl.BlockSpec((m, TILE), lambda j, sp: (base_at, j)))
    for pieces, weights in terms:
        for piece in pieces:
            for x in piece:
                args.append(x)
                specs.append(pl.BlockSpec(x.shape, lambda j, sp: (0, 0)))
        rows = sum(piece[0].shape[0] for piece in pieces)
        depth = pieces[0][0].shape[1]
        scratch.append(pltpu.VMEM((rows, depth), BF16))
        if isinstance(weights[0], tuple):
            args += [query_weight] * len(weights) + [kv_weight] * len(weights)
            specs += [own(at, size, TILE, True) for at, size in weights]
            specs += [own(at, size, kv_width, False) for at, size in weights]
            shape.append((tuple(len(p) for p in pieces), tuple(weights)))
        else:
            args += list(weights)
            specs += [pl.BlockSpec((w.shape[0], TILE), lambda j, sp: (0, j)) for w in weights]
            shape.append((tuple(len(p) for p in pieces), len(weights)))
    rows = [scratch[chosen[0]].shape[0] for chosen in sums]
    out = pl.pallas_call(
        functools.partial(
            product_kernel, shape, sums, kinds, (tiles, kv_width), base is not None
        ),
        out_shape=[jax.ShapeDtypeStruct((m, width + kv_width), k) for m in rows for k in kinds],
        grid_spec=pltpu.PrefetchScalarGridSpec(
            num_scalar_prefetch=1,
            grid=(tiles + 1,),
            in_specs=specs,
            out_specs=[pl.BlockSpec((m, TILE), lambda j, sp: (0, j)) for m in rows for _ in kinds],
            scratch_shapes=scratch,
        ),
        compiler_params=pltpu.CompilerParams(vmem_limit_bytes=60 * 2**20),
        cost_estimate=pl.CostEstimate(flops=10**10, bytes_accessed=10**6, transcendentals=0),
    )(sp, *args)
    out = [tuple(out[i : i + len(kinds)]) for i in range(0, len(out), len(kinds))]
    return out[0] if len(out) == 1 else out


def staged(tokens, query_weight, kv_weight):
    rows, depth = tokens.shape
    width = query_weight.shape[1]
    columns = width + kv_weight.shape[1]
    z, hid, grp = (lax.axis_index(name) for name in ("ffn", "hid", "grp"))
    chip, core = hid // 2, hid % 2
    part = depth * 5 // 36 // 128 * 128
    first = depth - 2 * part
    mid, into, out = along("ffn", MID), along("ffn", INTO), along("ffn", OUT)
    across = along("grp", [(0, 1), (1, 0)])
    own_at, far_at = first + grp * part, first + (1 - grp) * part
    inner = (z == 1) | (z == 2)
    sp = jnp.stack([inner, own_at, far_at]).astype(jnp.int32)
    weights1 = ((0, first),)
    weights2 = (((1,), part), ((2,), part))
    early_rows = rows * 15 // 32
    spans = ((0, early_rows), (early_rows, rows - early_rows))
    share = part // 2

    def at(x, i):
        return lax.dynamic_index_in_dim(x, i, keepdims=False)

    def from_plane(x, block):
        stage = 0
        for i, order in enumerate(ORDER):
            stage += i * (sum(jnp.where(z == k, b, 0) for k, b in enumerate(order)) == block)
        m = x.shape[0] // 4
        return lax.dynamic_slice_in_dim(x, stage * m, m, 0)

    def give_core(x):
        return jnp.stack([from_plane(x, 2 * i + 1 - core) for i in range(2)])

    def over_cores(x, got):
        keep = from_plane(x, hid) + at(got, chip).astype(F32)
        give = from_plane(x, hid ^ 2) + at(got, 1 - chip).astype(F32)
        return keep, give.astype(BF16)

    def shared_rows(parts):
        mine = gathered(jnp.concatenate([x[:, width:] for x in parts], 0))
        other = other_core(mine)
        return jnp.where(core == 0, mine, other), jnp.where(core == 0, other, mine)

    def mark(*xs):
        return sum(x[:16, :128] for x in xs)

    def weights_at(i):
        return jnp.concatenate(
            [
                lax.dynamic_slice_in_dim(w, own_at + i * share, share, 0)
                for w in (query_weight, kv_weight)
            ],
            1,
        )

    def shares(rest, w):
        return product(
            sp,
            query_weight,
            kv_weight,
            [([(x,) for x in rest], weights2), ([(x,) for x in rest], w)],
            ((0,), (1,)),
        )

    def whole(pieces, base):
        return product(
            sp, query_weight, kv_weight, [(pieces, weights1)], ((0,),), base=base
        )

    t1 = [tokens[a : a + m, :first] for a, m in spans]
    t2 = [
        jnp.concatenate(
            [lax.dynamic_slice(tokens, (a, i), (m, part)) for i in (own_at, far_at)], 1
        )
        for a, m in spans
    ]
    s = Steps()
    c2 = [s.start(into, x) for x in t2]
    b1 = [s.start(mid, t1[0])]
    e1 = [s.start(out, t1[0])]
    s.step()
    s.run(mark, c2[0], b1[0])
    w_in = [s.start(into, weights_at(0))]
    d2 = [s.start(mid, x) for x in c2]
    e1.append(s.start(out, t1[1]))
    s.step()
    s.run(mark, w_in[0], d2[0])
    w_in.append(s.start(into, weights_at(1)))
    b1.append(s.start(mid, t1[1]))
    f1 = [s.start(out, b1[0])]
    w_far = [s.start(across, w_in[0])]
    s.step()
    s.run(mark, w_in[1], b1[1])
    c1 = [s.start(into, t1[0])]
    b2 = [s.start(mid, x) for x in t2]
    f1.append(s.start(out, b1[1]))
    w_far.append(s.start(across, w_in[1]))
    s.step()
    s.run(mark, c1[0], b2[0])
    c1.append(s.start(into, t1[1]))
    d1 = [s.start(mid, c1[0])]
    rest = [[jnp.where(inner, x, jnp.zeros_like(x)), *y] for x, *y in zip(t2, b2, c2, d2)]
    w_help = w_in + w_far

    def complete(x, y):
        return (x + y.astype(F32)).astype(BF16)

    def finished(q, got, o):
        return (q + got.astype(F32) + o.astype(F32)).astype(BF16)

    def block(i, after=None):
        b, e, c, f, d, g = gate([y[i] for y in (b1, e1, c1, f1, d1, g1)], (after,))
        return [(t1[i],), (b, e), (c, f), (d, g)]

    (p0, _), (h0, h0_16) = s.run(shares, rest[0], w_help)
    s.step()
    s.run(mark, c1[1], d1[0])
    d1.append(s.start(mid, c1[1]))
    g1 = [s.start(out, d1[0])]
    (h0_16,) = gate((h0_16,), (s.last,))
    h0_core = s.start(other_core, give_core(h0_16))
    h0, h0_give = s.run(over_cores, h0, h0_core)
    h0_got = s.start(other_chip, h0_give)
    (p1, _), (h1, h1_16) = s.run(shares, rest[1], w_help)
    s.step()
    h0 = s.run(complete, h0, h0_got)
    g1.append(s.start(out, d1[1]))
    o0 = s.start(out, h0, 2)
    (h1_16,) = gate((h1_16,), (s.last,))
    h1_core = s.start(other_core, give_core(h1_16))
    h1, h1_give = s.run(over_cores, h1, h1_core)
    h1_got = s.start(other_chip, h1_give)
    q0, q0_16 = s.run(whole, block(0, h1_give), p0)
    s.step()
    h1 = s.run(complete, h1, h1_got)
    o1 = s.start(out, h1, 9)
    q0_core = s.start(other_core, give_core(q0_16))
    q0, q0_give = s.run(over_cores, q0, q0_core)
    q0_got = s.start(other_chip, q0_give)
    q1, q1_16 = s.run(whole, block(1, q0_give), p1)
    s.step()
    q0 = s.run(finished, q0, q0_got, o0)
    q1_core = s.start(other_core, give_core(q1_16))
    q1, q1_give = s.run(over_cores, q1, q1_core)
    q1_got = other_chip(q1_give)
    early = shared_rows([q0])
    q1 = finished(q1, q1_got, o1)
    queries = jnp.concatenate([x[:, :width] for x in (q0, q1)], 0)
    late = shared_rows([q1])
    shared = jnp.concatenate([early[0], late[0], early[1], late[1]], 0)
    return attention(core, queries, shared)


def solution(mesh):
    fits = mesh.shape["ffn"] == 4 and mesh.shape["hid"] == 4 and mesh.shape["grp"] == 2
    return jax.shard_map(
        staged if fits else general,
        mesh=mesh,
        in_specs=(P(("grp", "ffn"), "hid"), P("hid", "ffn"), P("hid", "ffn")),
        out_specs=P(("grp", "hid"), "ffn"),
        check_vma=False,
    )
```
